128 devices in a mesh: dp: 8 (over y, x_hi), row: 4 (over z), col: 4 (over x_lo, core).
Axes of the slice: x: 4 (x_hi: 2, x_lo: 2; x = x_hi * 2 + x_lo), y: 4, z: 4, core: 2. Of those that a mesh axis runs over, the one named last changes fastest.
Arguments:
- hidden: bfloat16 [8192, 6656], P(('dp', 'row'), 'col'), may hold values from -6 to 6
- weight: bfloat16 [6656, 8192], P('row', 'col'), may hold values from -0.078125 to 0.078125
- upstream: bfloat16 [8192, 8192], P(('dp', 'row'), 'col'), may hold values from -6 to 6
Outputs:
- output: bfloat16 [8192, 8192], P(('dp', 'row'), 'col')
- hidden_grad: bfloat16 [8192, 6656], P(('dp', 'row'), 'col')
- weight_grad: float32 [6656, 8192], P(('row', 'dp'), 'col')
The draws below stay inside these ranges and needn't reach their ends.
All inputs are finite; a program needn't handle non-finite values.
Results may differ from the reference program's by a relative error of at most 0.015.
Values may be sent and summed in bfloat16 or wider, within the bound.
No kernel may reach another device: no remote copies, remote signals or barrier semaphores. Data moves between devices by JAX's collectives and lax.ppermute only.
A program may use at most 192 MiB of HBM per device.

```python
import math
import jax
import jax.numpy as jnp

D = 8192
F = 6656
TOK_DEV = 256
TOKENS = 8192
N_DP = 8
N_ROW = 4


def block_levels(key, shape, split, least, largest):
    level = 1.0
    for axis_at, shards_of in split:
        steps = jax.random.uniform(jax.random.fold_in(jax.random.fold_in(key, 6), axis_at), (shards_of,), jnp.float32, least / len(split), largest / len(split))
        level = level * jnp.repeat(jnp.exp(steps), shape[axis_at] // shards_of).reshape((-1,) + (1,) * (len(shape) - 1 - axis_at))
    return level


def centred(key, extent, deviation, most, shards=(), dtype=jnp.bfloat16):
    entries = jax.random.normal(key, extent, jnp.float32) * deviation
    if len(shards) > 0:
        entries = block_levels(key, extent, shards, -0.22, 0.18) * entries
    return jnp.clip(entries, min=-most, max=most).astype(dtype)


def setup_inputs(seed: int = 0) -> dict:
    streams_of = jax.random.split(jax.random.key(seed), 4)
    return {
        "hidden": centred(streams_of[0], (TOKENS, F), 1.0, 6.0, ((0, 32), (1, 4))),
        "weight": centred(streams_of[1], (F, D), F ** -0.5, 0.078125, ((0, 4), (1, 4))),
        "upstream": centred(streams_of[2], (TOKENS, D), 1.0, 6.0, ((0, 32), (1, 4))),
    }


def reference(hidden, weight, upstream):
    output = jnp.dot(hidden, weight, preferred_element_type=jnp.float32).astype(jnp.bfloat16)
    hidden_grad = jnp.dot(upstream, weight.T, preferred_element_type=jnp.float32).astype(jnp.bfloat16)
    replica_rows = TOK_DEV * N_ROW
    factor = 1.0 / math.sqrt(TOKENS)
    total = jnp.zeros((F, D), jnp.float32)
    for replica in range(N_DP):
        left = hidden[replica * replica_rows:(replica + 1) * replica_rows]
        right = upstream[replica * replica_rows:(replica + 1) * replica_rows]
        partial_grad = jnp.dot(left.T, right, preferred_element_type=jnp.float32) * factor
        total = total + partial_grad.astype(jnp.bfloat16).astype(jnp.float32)
    return (output, hidden_grad, total)
```

```python
import math

import jax
import jax.numpy as jnp
from jax import lax
from jax.sharding import PartitionSpec as P

BF = jnp.bfloat16
F32 = jnp.float32
Z_UP = [(i, (i + 1) % 4) for i in range(4)]
Z_DOWN = [(i, (i + 3) % 4) for i in range(4)]
Y_UP = [(i, (i + 2) % 8) for i in range(8)]
Y_DOWN = [(i, (i + 6) % 8) for i in range(8)]
XHI = [(i, i ^ 1) for i in range(8)]
XLO = [(i, i ^ 2) for i in range(4)]
CORE = [(i, i ^ 1) for i in range(4)]
TO_PLANE = [(t * 4 + f, f * 4 + (t - f) % 4) for t in range(4) for f in range(4)]
FROM_PLANE = [(b, a) for a, b in TO_PLANE]


def dot(a, b, ca, cb):
    return lax.dot_general(a, b, (((ca,), (cb,)), ((), ())), preferred_element_type=F32)


def at(a, i):
    return lax.dynamic_index_in_dim(a, i, 0, keepdims=False)


def pair(first, own, other):
    both = jnp.zeros((2,) + own.shape, own.dtype)
    both = lax.dynamic_update_index_in_dim(both, own, first, 0)
    return lax.dynamic_update_index_in_dim(both, other, 1 - first, 0)


def shards(hidden, weight, upstream):
    d, c = lax.axis_index("dp"), lax.axis_index("col")
    y, xhi, xlo, core = d // 2, d % 2, c // 2, c % 2
    rows, f = hidden.shape
    w = upstream.shape[1]
    half = rows // 2

    h_own = lax.ppermute(hidden, ("row", "col"), TO_PLANE)
    h_x = lax.ppermute(h_own, "col", XLO)
    h_two = pair(xlo, h_own, h_x)
    h_c = lax.ppermute(h_two, "col", CORE)
    h = pair(core, h_two, h_c)
    h = jnp.swapaxes(h, 0, 1).reshape(4 * rows, f)

    u3 = lax.ppermute(upstream, "row", Z_UP)
    u1 = lax.ppermute(upstream, "row", Z_DOWN)
    u2a = lax.ppermute(u3[:half], "row", Z_UP)
    u2b = lax.ppermute(u1[half:], "row", Z_DOWN)
    u = jnp.concatenate([upstream, u1, u2a, u2b, u3], axis=0)

    token_count = lax.axis_size("dp") * lax.axis_size("row") * rows
    factor = 1.0 / math.sqrt(token_count)
    wg = (dot(h, u, 0, 0) * factor).astype(BF).reshape(4, f // 4, w)
    hf = f // 8
    w2 = at(wg, (y + 2) % 4)
    w1 = at(wg, (y + 1) % 4)
    w3 = at(wg, (y + 3) % 4)
    wa = lax.ppermute(w2[:hf], "dp", Y_UP)
    wb = lax.ppermute(w2[hf:], "dp", Y_DOWN)
    s1b = lax.ppermute(w1[hf:], "dp", Y_UP)
    s3a = lax.ppermute(w3[:hf], "dp", Y_DOWN)
    s1a = lax.ppermute((w1[:hf].astype(F32) + wa.astype(F32)).astype(BF), "dp", Y_UP)
    s3b = lax.ppermute((w3[hf:].astype(F32) + wb.astype(F32)).astype(BF), "dp", Y_DOWN)
    w0 = at(wg, y).astype(F32)
    t_a = w0[:hf] + s1a.astype(F32) + s3a.astype(F32)
    t_b = w0[hf:] + s1b.astype(F32) + s3b.astype(F32)
    low = xhi == 0
    x_in = lax.ppermute(jnp.where(low, t_b, t_a).astype(BF), "dp", XHI)
    weight_grad = jnp.where(low, t_a, t_b) + x_in.astype(F32)

    hk = [h[k * rows : (k + 1) * rows] for k in range(4)]
    o2 = dot(hk[2], weight, 1, 0).astype(BF)
    oa = lax.ppermute(o2[:half], "row", Z_UP)
    ob = lax.ppermute(o2[half:], "row", Z_DOWN)
    o1 = dot(hk[1], weight, 1, 0)
    o3 = dot(hk[3], weight, 1, 0)
    o1 = jnp.concatenate([o1[:half] + oa.astype(F32), o1[half:]], axis=0).astype(BF)
    o3 = jnp.concatenate([o3[:half], o3[half:] + ob.astype(F32)], axis=0).astype(BF)
    from_below = lax.ppermute(o1, "row", Z_UP)
    from_above = lax.ppermute(o3, "row", Z_DOWN)
    output = (
        dot(hk[0], weight, 1, 0) + from_below.astype(F32) + from_above.astype(F32)
    ).astype(BF)

    ux = jnp.swapaxes(u.reshape(2, 2, rows, w), 0, 1)
    g_send = dot(at(ux, 1 - core).reshape(2 * rows, w), weight, 1, 1).astype(BF)
    g_in = lax.ppermute(g_send, "col", CORE)
    g = dot(at(ux, core).reshape(2 * rows, w), weight, 1, 1) + g_in.astype(F32)
    g = g.reshape(2, rows, f)
    g_x = lax.ppermute(at(g, 1 - xlo).astype(BF), "col", XLO)
    g = (at(g, xlo) + g_x.astype(F32)).astype(BF)
    hidden_grad = lax.ppermute(g, ("row", "col"), FROM_PLANE)
    return (output, hidden_grad, weight_grad)


def solution(mesh):
    return jax.shard_map(
        shards,
        mesh=mesh,
        in_specs=(P(("dp", "row"), "col"), P("row", "col"), P(("dp", "row"), "col")),
        out_specs=(P(("dp", "row"), "col"), P(("dp", "row"), "col"), P(("row", "dp"), "col")),
        check_vma=False,
    )
```

```python
import math

import jax
import jax.numpy as jnp
from jax import lax
from jax.experimental import pallas as pl
from jax.experimental.pallas import tpu as pltpu
from jax.sharding import PartitionSpec as P

BF = jnp.bfloat16
F32 = jnp.float32
Z_UP = [(i, (i + 1) % 4) for i in range(4)]
Z_DOWN = [(i, (i + 3) % 4) for i in range(4)]
Y_UP = [(i, (i + 2) % 8) for i in range(8)]
Y_DOWN = [(i, (i + 6) % 8) for i in range(8)]
XHI = [(i, i ^ 1) for i in range(8)]
XLO = [(i, i ^ 2) for i in range(4)]
CORE = [(i, i ^ 1) for i in range(4)]
TO_PLANE = [(t * 4 + f, f * 4 + (t - f) % 4) for t in range(4) for f in range(4)]
TO_PLANE_X = [(a, b ^ 2) for a, b in TO_PLANE]
FROM_PLANE = [(b, a) for a, b in TO_PLANE]
FROM_PLANE_X = [(b, a) for a, b in TO_PLANE_X]
CHUNKS = ((0, 1024), (1024, 2048))


def dot(a, b, ca, cb):
    return lax.dot_general(a, b, (((ca,), (cb,)), ((), ())), preferred_element_type=F32)


def at(a, i):
    return lax.dynamic_index_in_dim(a, i, 0, keepdims=False)


def params(mib):
    return pltpu.CompilerParams(vmem_limit_bytes=mib * 1024 * 1024)


COST = pl.CostEstimate(flops=1000, bytes_accessed=1000, transcendentals=0)


def tokens_by_width(place, hs, w, block=256):
    def kernel(place_ref, *refs):
        w_ref, o_ref = refs[-2:]
        o = dot(jnp.concatenate([r[...] for r in refs[:-2]], axis=0), w_ref[...], 1, 0).astype(BF)
        rows = o_ref.shape[1]
        for k in range(4):
            o_ref[lax.rem(place_ref[0] + k, 4)] = o[k * rows : (k + 1) * rows]

    rows, n = hs[0].shape[0], w.shape[1]
    return pl.pallas_call(
        kernel,
        grid_spec=pltpu.PrefetchScalarGridSpec(
            num_scalar_prefetch=1,
            grid=(n // block,),
            in_specs=[pl.BlockSpec(h.shape, lambda i, p: (0, 0), pipeline_mode=pl.Buffered(1)) for h in hs]
            + [pl.BlockSpec((w.shape[0], block), lambda i, p: (0, i))],
            out_specs=pl.BlockSpec((4, rows, block), lambda i, p: (0, 0, i)),
        ),
        out_shape=jax.ShapeDtypeStruct((4, rows, n), BF),
        cost_estimate=COST,
        compiler_params=params(16),
    )(place, *hs, w)


def after(token, *values):
    return lax.optimization_barrier((token,) + values)[1:]


def shards(hidden, weight, upstream):
    z, d, c = lax.axis_index("row"), lax.axis_index("dp"), lax.axis_index("col")
    y, xhi, xlo, core = d // 2, d % 2, c // 2, c % 2
    rows, f = hidden.shape
    half = rows // 2
    left, even, low = xlo == 0, core == 0, xhi == 0

    own_a = lax.ppermute(hidden[:half], ("row", "col"), TO_PLANE)
    own_b = lax.ppermute(hidden[half:], ("row", "col"), TO_PLANE_X)
    u3 = lax.ppermute(upstream, "row", Z_UP)
    u1 = lax.ppermute(upstream, "row", Z_DOWN)
    g0 = dot(upstream, weight, 1, 1).astype(BF)
    own = jnp.stack([own_a, own_b])
    swapped = lax.ppermute(own, "col", XLO)
    two = jnp.stack(
        [
            jnp.where(left, own_a, swapped[0]),
            jnp.where(left, swapped[1], own_b),
            jnp.where(left, swapped[0], own_a),
            jnp.where(left, own_b, swapped[1]),
        ]
    ).reshape(2, rows, f)
    other = lax.ppermute(two, "col", CORE)
    hs = (
        jnp.where(even, two[0], other[0]),
        jnp.where(even, other[0], two[0]),
        jnp.where(even, two[1], other[1]),
        jnp.where(even, other[1], two[1]),
    )

    u2a = lax.ppermute(u3[:half], "row", Z_UP)
    u2b = lax.ppermute(u1[half:], "row", Z_DOWN)
    g1, g3 = dot(u1, weight, 1, 1).astype(BF), dot(u3, weight, 1, 1).astype(BF)

    o = tokens_by_width(jnp.reshape(z, (1,)).astype(jnp.int32), hs, weight)
    o_in = lax.all_to_all(o, "row", 0, 0, tiled=True)

    u2a, u2b = after(o, u2a, u2b)
    g2 = dot(jnp.concatenate([u2a, u2b], axis=0), weight, 1, 1).astype(BF)
    g_send = jnp.stack([jnp.where(even, g1, g0), jnp.where(even, g3, g2)])
    g_in = lax.ppermute(g_send, "col", CORE)
    hs = after(g_send, *hs)

    token_count = lax.axis_size("dp") * lax.axis_size("row") * rows
    factor = 1.0 / math.sqrt(token_count)
    hf = f // 8
    near, was, wbs = [], [], []
    u = jnp.concatenate([upstream, u1, u2a, u2b, u3], axis=0)
    for lo, hi in CHUNKS:
        wg = (dot(jnp.concatenate(hs, axis=0), u[:, lo:hi], 0, 0) * factor).astype(BF)
        wg = wg.reshape(4, f // 4, hi - lo)
        w2 = at(wg, (y + 2) % 4)
        w2a, w2b = w2[:hf], w2[hf:]
        rest = [at(wg, (y + 1) % 4), at(wg, (y + 3) % 4), at(wg, y)]
        hs = after(w2a, *hs)
        was.append(lax.ppermute(w2a, "dp", Y_UP))
        wbs.append(lax.ppermute(w2b, "dp", Y_DOWN))
        near.append(rest)

    def second(i):
        w1, w3, _ = near[i]
        w1 = lax.dynamic_update_slice(w1, (w1[:hf].astype(F32) + was[i].astype(F32)).astype(BF), (0, 0))
        w3 = lax.dynamic_update_slice(w3, (w3[hf:].astype(F32) + wbs[i].astype(F32)).astype(BF), (hf, 0))
        w1, w3 = lax.optimization_barrier((w1, w3))
        return w1, w3, lax.ppermute(w1, "dp", Y_UP), lax.ppermute(w3, "dp", Y_DOWN)

    was[0], wbs[0] = after(w2a, was[0], wbs[0])
    w1, w3, s1, s3 = second(0)

    (g_in,) = after(w3, g_in)
    g0 = jnp.where(even, g0, g1).astype(F32) + g_in[0].astype(F32)
    g1 = jnp.where(even, g2, g3).astype(F32) + g_in[1].astype(F32)
    keep_a, keep_b = jnp.where(left, g0[:half], g1[:half]), jnp.where(left, g1[half:], g0[half:])
    send = jnp.stack([jnp.where(left, g1[:half], g0[:half]), jnp.where(left, g0[half:], g1[half:])])
    send = send.astype(BF)
    g_x = lax.ppermute(send, "col", XLO)

    was[1], wbs[1] = after(send, was[1], wbs[1])
    w1, w3, v1, v3 = second(1)

    def over_x(i, s1, s3):
        t = near[i][2].astype(F32) + s1.astype(F32) + s3.astype(F32)
        out = jnp.where(low, t[hf:], t[:hf]).astype(BF)
        return out, jnp.where(low, t[:hf], t[hf:]), lax.ppermute(out, "dp", XHI)

    s1, s3 = after(w3, s1, s3)
    x_out, mine0, x0 = over_x(0, s1, s3)

    (g_x,) = after(x_out, g_x)
    g_a, g_b = (keep_a + g_x[0].astype(F32)).astype(BF), (keep_b + g_x[1].astype(F32)).astype(BF)
    h_a = lax.ppermute(g_a, ("row", "col"), FROM_PLANE)
    h_b = lax.ppermute(g_b, ("row", "col"), FROM_PLANE_X)

    v1, v3 = after(g_b, v1, v3)
    x_out, mine1, x1 = over_x(1, v1, v3)

    (o_in,) = after(x_out, o_in)
    output = jnp.sum(o_in.astype(F32), axis=0).astype(BF)

    weight_grad = jnp.concatenate([mine0 + x0.astype(F32), mine1 + x1.astype(F32)], axis=1)
    hidden_grad = jnp.concatenate([h_a, h_b], axis=0)
    return (output, hidden_grad, weight_grad)


def solution(mesh):
    return jax.shard_map(
        shards,
        mesh=mesh,
        in_specs=(P(("dp", "row"), "col"), P("row", "col"), P(("dp", "row"), "col")),
        out_specs=(P(("dp", "row"), "col"), P(("dp", "row"), "col"), P(("row", "dp"), "col")),
        check_vma=False,
    )
```

```python
import math

import jax
import jax.numpy as jnp
from jax import lax
from jax.experimental import pallas as pl
from jax.experimental.pallas import tpu as pltpu
from jax.sharding import PartitionSpec as P

BF = jnp.bfloat16
F32 = jnp.float32
Z_UP = [(i, (i + 1) % 4) for i in range(4)]
Z_DOWN = [(i, (i + 3) % 4) for i in range(4)]
Y_UP = [(i, (i + 2) % 8) for i in range(8)]
Y_DOWN = [(i, (i + 6) % 8) for i in range(8)]
XHI = [(i, i ^ 1) for i in range(8)]
XLO = [(i, i ^ 2) for i in range(4)]
CORE = [(i, i ^ 1) for i in range(4)]
TO_PLANE = [(t * 4 + f, f * 4 + (t - f) % 4) for t in range(4) for f in range(4)]
TO_PLANE_X = [(a, b ^ 2) for a, b in TO_PLANE]
FROM_PLANE = [(b, a) for a, b in TO_PLANE]
FROM_PLANE_X = [(b, a) for a, b in TO_PLANE_X]
CHUNKS = ((0, 1024), (1024, 2048))


def dot(a, b, ca, cb):
    return lax.dot_general(a, b, (((ca,), (cb,)), ((), ())), preferred_element_type=F32)


def at(a, i):
    return lax.dynamic_index_in_dim(a, i, 0, keepdims=False)


def params(mib):
    return pltpu.CompilerParams(vmem_limit_bytes=mib * 1024 * 1024)


COST = pl.CostEstimate(flops=1000, bytes_accessed=1000, transcendentals=0)


def tokens_by_width(place, hs, w, block=512):
    def kernel(place_ref, *refs):
        w_ref, o_ref = refs[-2:]
        o = dot(jnp.concatenate([r[...] for r in refs[:-2]], axis=0), w_ref[...], 1, 0).astype(BF)
        rows = o_ref.shape[1]
        for k in range(4):
            o_ref[lax.rem(place_ref[0] + k, 4)] = o[k * rows : (k + 1) * rows]

    rows, n = hs[0].shape[0], w.shape[1]
    return pl.pallas_call(
        kernel,
        grid_spec=pltpu.PrefetchScalarGridSpec(
            num_scalar_prefetch=1,
            grid=(n // block,),
            in_specs=[pl.BlockSpec(h.shape, lambda i, p: (0, 0), pipeline_mode=pl.Buffered(1)) for h in hs]
            + [pl.BlockSpec((w.shape[0], block), lambda i, p: (0, i))],
            out_specs=pl.BlockSpec((4, rows, block), lambda i, p: (0, 0, i)),
        ),
        out_shape=jax.ShapeDtypeStruct((4, rows, n), BF),
        cost_estimate=COST,
        compiler_params=params(24),
    )(place, *hs, w)


def after(token, *values):
    return lax.optimization_barrier((token,) + values)[1:]


def shards(hidden, weight, upstream):
    z, d, c = lax.axis_index("row"), lax.axis_index("dp"), lax.axis_index("col")
    y, xhi, xlo, core = d // 2, d % 2, c // 2, c % 2
    rows, f = hidden.shape
    half = rows // 2
    left, even, low = xlo == 0, core == 0, xhi == 0

    own_a = lax.ppermute(hidden[:half], ("row", "col"), TO_PLANE)
    own_b = lax.ppermute(hidden[half:], ("row", "col"), TO_PLANE_X)
    u3 = lax.ppermute(upstream, "row", Z_UP)
    u1 = lax.ppermute(upstream, "row", Z_DOWN)
    g0 = dot(upstream, weight, 1, 1).astype(BF)
    own = jnp.stack([own_a, own_b])
    swapped = lax.ppermute(own, "col", XLO)
    two = jnp.stack(
        [
            jnp.where(left, own_a, swapped[0]),
            jnp.where(left, swapped[1], own_b),
            jnp.where(left, swapped[0], own_a),
            jnp.where(left, own_b, swapped[1]),
        ]
    ).reshape(2, rows, f)
    other = lax.ppermute(two, "col", CORE)
    hs = (
        jnp.where(even, two[0], other[0]),
        jnp.where(even, other[0], two[0]),
        jnp.where(even, two[1], other[1]),
        jnp.where(even, other[1], two[1]),
    )

    u2a = lax.ppermute(u3[:half], "row", Z_UP)
    u2b = lax.ppermute(u1[half:], "row", Z_DOWN)
    g1, g3 = dot(u1, weight, 1, 1).astype(BF), dot(u3, weight, 1, 1).astype(BF)

    o = tokens_by_width(jnp.reshape(z, (1,)).astype(jnp.int32), hs, weight)
    o_in = lax.all_to_all(o, "row", 0, 0, tiled=True)

    u2a, u2b = after(o, u2a, u2b)
    g2 = dot(jnp.concatenate([u2a, u2b], axis=0), weight, 1, 1).astype(BF)
    g_send = jnp.stack([jnp.where(even, g1, g0), jnp.where(even, g3, g2)])
    g_in = lax.ppermute(g_send, "col", CORE)
    hs = after(g_send, *hs)

    token_count = lax.axis_size("dp") * lax.axis_size("row") * rows
    factor = 1.0 / math.sqrt(token_count)
    hf = f // 8
    near, was, wbs = [], [], []
    u = jnp.concatenate([upstream, u1, u2a, u2b, u3], axis=0)
    for lo, hi in CHUNKS:
        wg = (dot(jnp.concatenate(hs, axis=0), u[:, lo:hi], 0, 0) * factor).astype(BF)
        wg = wg.reshape(4, f // 4, hi - lo)
        w2 = at(wg, (y + 2) % 4)
        w2a, w2b = w2[:hf], w2[hf:]
        rest = [at(wg, (y + 1) % 4), at(wg, (y + 3) % 4), at(wg, y)]
        hs = after(w2a, *hs)
        was.append(lax.ppermute(w2a, "dp", Y_UP))
        wbs.append(lax.ppermute(w2b, "dp", Y_DOWN))
        near.append(rest)

    def second(i):
        w1, w3, _ = near[i]
        w1 = lax.dynamic_update_slice(w1, (w1[:hf].astype(F32) + was[i].astype(F32)).astype(BF), (0, 0))
        w3 = lax.dynamic_update_slice(w3, (w3[hf:].astype(F32) + wbs[i].astype(F32)).astype(BF), (hf, 0))
        w1, w3 = lax.optimization_barrier((w1, w3))
        return w1, w3, lax.ppermute(w1, "dp", Y_UP), lax.ppermute(w3, "dp", Y_DOWN)

    was[0], wbs[0] = after(w2a, was[0], wbs[0])
    w1, w3, s1, s3 = second(0)

    (g_in,) = after(w3, g_in)
    g0 = jnp.where(even, g0, g1).astype(F32) + g_in[0].astype(F32)
    g1 = jnp.where(even, g2, g3).astype(F32) + g_in[1].astype(F32)
    keep_a, keep_b = jnp.where(left, g0[:half], g1[:half]), jnp.where(left, g1[half:], g0[half:])
    send = jnp.stack([jnp.where(left, g1[:half], g0[:half]), jnp.where(left, g0[half:], g1[half:])])
    send = send.astype(BF)
    g_x = lax.ppermute(send, "col", XLO)

    was[1], wbs[1] = after(send, was[1], wbs[1])
    w1, w3, v1, v3 = second(1)

    def over_x(i, s1, s3):
        t = near[i][2].astype(F32) + s1.astype(F32) + s3.astype(F32)
        out = jnp.where(low, t[hf:], t[:hf]).astype(BF)
        return out, jnp.where(low, t[:hf], t[hf:]), lax.ppermute(out, "dp", XHI)

    s1, s3 = after(w3, s1, s3)
    x_out, mine0, x0 = over_x(0, s1, s3)

    (g_x,) = after(x_out, g_x)
    g_a, g_b = (keep_a + g_x[0].astype(F32)).astype(BF), (keep_b + g_x[1].astype(F32)).astype(BF)
    h_a = lax.ppermute(g_a, ("row", "col"), FROM_PLANE)
    h_b = lax.ppermute(g_b, ("row", "col"), FROM_PLANE_X)

    (o_in,) = after(g_b, o_in)
    output = jnp.sum(o_in.astype(F32), axis=0).astype(BF)

    v1, v3 = after(output, v1, v3)
    x_out, mine1, x1 = over_x(1, v1, v3)

    weight_grad = jnp.concatenate([mine0 + x0.astype(F32), mine1 + x1.astype(F32)], axis=1)
    hidden_grad = jnp.concatenate([h_a, h_b], axis=0)
    return (output, hidden_grad, weight_grad)


def solution(mesh):
    return jax.shard_map(
        shards,
        mesh=mesh,
        in_specs=(P(("dp", "row"), "col"), P("row", "col"), P(("dp", "row"), "col")),
        out_specs=(P(("dp", "row"), "col"), P(("dp", "row"), "col"), P(("row", "dp"), "col")),
        check_vma=False,
    )
```

```python
import math

import jax
import jax.numpy as jnp
from jax import lax
from jax.experimental import pallas as pl
from jax.experimental.pallas import tpu as pltpu
from jax.sharding import PartitionSpec as P

BF = jnp.bfloat16
F32 = jnp.float32
Z_UP = [(i, (i + 1) % 4) for i in range(4)]
Z_DOWN = [(i, (i + 3) % 4) for i in range(4)]
Y_UP = [(i, (i + 2) % 8) for i in range(8)]
Y_DOWN = [(i, (i + 6) % 8) for i in range(8)]
XHI = [(i, i ^ 1) for i in range(8)]
XLO = [(i, i ^ 2) for i in range(4)]
CORE = [(i, i ^ 1) for i in range(4)]
TO_PLANE = [(t * 4 + f, f * 4 + (t - f) % 4) for t in range(4) for f in range(4)]
TO_PLANE_X = [(a, b ^ 2) for a, b in TO_PLANE]
FROM_PLANE = [(b, a) for a, b in TO_PLANE]
CHUNKS = ((0, 1024), (1024, 2048))


def dot(a, b, ca, cb):
    return lax.dot_general(a, b, (((ca,), (cb,)), ((), ())), preferred_element_type=F32)


def at(a, i):
    return lax.dynamic_index_in_dim(a, i, 0, keepdims=False)


def params(mib):
    return pltpu.CompilerParams(vmem_limit_bytes=mib * 1024 * 1024)


COST = pl.CostEstimate(flops=1000, bytes_accessed=1000, transcendentals=0)


def tokens_by_width(place, hs, w, block=512):
    def kernel(place_ref, *refs):
        w_ref, o_ref = refs[-2:]
        o = dot(jnp.concatenate([r[...] for r in refs[:-2]], axis=0), w_ref[...], 1, 0).astype(BF)
        rows = o_ref.shape[1]
        for k in range(4):
            o_ref[lax.rem(place_ref[0] + k, 4)] = o[k * rows : (k + 1) * rows]

    rows, n = hs[0].shape[0], w.shape[1]
    return pl.pallas_call(
        kernel,
        grid_spec=pltpu.PrefetchScalarGridSpec(
            num_scalar_prefetch=1,
            grid=(n // block,),
            in_specs=[pl.BlockSpec(h.shape, lambda i, p: (0, 0), pipeline_mode=pl.Buffered(1)) for h in hs]
            + [pl.BlockSpec((w.shape[0], block), lambda i, p: (0, i))],
            out_specs=pl.BlockSpec((4, rows, block), lambda i, p: (0, 0, i)),
        ),
        out_shape=pltpu.HBM((4, rows, n), BF),
        cost_estimate=COST,
        compiler_params=params(24),
    )(place, *hs, w)


def after(token, *values):
    return lax.optimization_barrier((token,) + values)[1:]


def shards(hidden, weight, upstream):
    z, d, c = lax.axis_index("row"), lax.axis_index("dp"), lax.axis_index("col")
    y, xhi, xlo, core = d // 2, d % 2, c // 2, c % 2
    rows, f = hidden.shape
    half = rows // 2
    left, even, low = xlo == 0, core == 0, xhi == 0

    own_a = lax.ppermute(hidden[:half], ("row", "col"), TO_PLANE)
    own_b = lax.ppermute(hidden[half:], ("row", "col"), TO_PLANE_X)
    (upstream,) = after(own_a, upstream)
    u3 = lax.ppermute(upstream, "row", Z_UP)
    u1 = lax.ppermute(upstream, "row", Z_DOWN)
    g0 = dot(upstream, weight, 1, 1).astype(BF)
    own = jnp.stack([own_a, own_b])
    swapped = lax.ppermute(own, "col", XLO)
    two = jnp.stack(
        [
            jnp.where(left, own_a, swapped[0]),
            jnp.where(left, swapped[1], own_b),
            jnp.where(left, swapped[0], own_a),
            jnp.where(left, own_b, swapped[1]),
        ]
    ).reshape(2, rows, f)
    other = lax.ppermute(two, "col", CORE)
    hs = (
        jnp.where(even, two[0], other[0]),
        jnp.where(even, other[0], two[0]),
        jnp.where(even, two[1], other[1]),
        jnp.where(even, other[1], two[1]),
    )

    u2a = lax.ppermute(u3[:half], "row", Z_UP)
    u2b = lax.ppermute(u1[half:], "row", Z_DOWN)
    g1, g3 = dot(u1, weight, 1, 1).astype(BF), dot(u3, weight, 1, 1).astype(BF)

    g2 = dot(jnp.concatenate([u2a, u2b], axis=0), weight, 1, 1).astype(BF)
    g_send = jnp.stack([jnp.where(even, g1, g0), jnp.where(even, g3, g2)])
    g_in = lax.ppermute(g_send, "col", CORE)
    hs = after(g_send, *hs)

    token_count = lax.axis_size("dp") * lax.axis_size("row") * rows
    factor = 1.0 / math.sqrt(token_count)
    hf = f // 8
    near, was, wbs = [], [], []
    u = jnp.concatenate([upstream, u1, u2a, u2b, u3], axis=0)
    for lo, hi in CHUNKS:
        wg = (dot(jnp.concatenate(hs, axis=0), u[:, lo:hi], 0, 0) * factor).astype(BF)
        wg = wg.reshape(4, f // 4, hi - lo)
        w2 = at(wg, (y + 2) % 4)
        w2a, w2b = w2[:hf], w2[hf:]
        rest = [at(wg, (y + 1) % 4), at(wg, (y + 3) % 4), at(wg, y)]
        hs = after(w2a, *hs)
        was.append(lax.ppermute(w2a, "dp", Y_UP))
        wbs.append(lax.ppermute(w2b, "dp", Y_DOWN))
        near.append(rest)

    def second(i):
        w1, w3, _ = near[i]
        w1 = lax.dynamic_update_slice(w1, (w1[:hf].astype(F32) + was[i].astype(F32)).astype(BF), (0, 0))
        w3 = lax.dynamic_update_slice(w3, (w3[hf:].astype(F32) + wbs[i].astype(F32)).astype(BF), (hf, 0))
        w1, w3 = lax.optimization_barrier((w1, w3))
        return w1, w3, lax.ppermute(w1, "dp", Y_UP), lax.ppermute(w3, "dp", Y_DOWN)

    o = tokens_by_width(jnp.reshape(z, (1,)).astype(jnp.int32), hs, weight)
    o, was[0], wbs[0] = lax.optimization_barrier((o, was[0], wbs[0]))
    w1, w3, s1, s3 = second(0)
    (o,) = after(w3, o)
    o_in = lax.all_to_all(o, "row", 0, 0, tiled=True)

    (g_in,) = after(w3, g_in)
    g0 = jnp.where(even, g0, g1).astype(F32) + g_in[0].astype(F32)
    g1 = jnp.where(even, g2, g3).astype(F32) + g_in[1].astype(F32)
    send = jnp.where(left, g1, g0).astype(BF)
    g_x = lax.ppermute(send, "col", XLO)

    was[1], wbs[1] = after(send, was[1], wbs[1])
    w1, w3, v1, v3 = second(1)

    def over_x(i, s1, s3):
        t = near[i][2].astype(F32) + s1.astype(F32) + s3.astype(F32)
        out = jnp.where(low, t[hf:], t[:hf]).astype(BF)
        return out, jnp.where(low, t[:hf], t[hf:]), lax.ppermute(out, "dp", XHI)

    s1, s3 = after(w3, s1, s3)
    x_out, mine0, x0 = over_x(0, s1, s3)

    (g_x,) = after(x_out, g_x)
    g_b = (jnp.where(left, g0, g1) + g_x.astype(F32)).astype(BF)
    hidden_grad = lax.ppermute(g_b, ("row", "col"), FROM_PLANE)

    v1, v3 = after(g_b, v1, v3)
    x_out, mine1, x1 = over_x(1, v1, v3)

    (o_in,) = after(x_out, o_in)
    output = jnp.sum(o_in.astype(F32), axis=0).astype(BF)

    weight_grad = jnp.concatenate([mine0 + x0.astype(F32), mine1 + x1.astype(F32)], axis=1)
    return (output, hidden_grad, weight_grad)


def solution(mesh):
    return jax.shard_map(
        shards,
        mesh=mesh,
        in_specs=(P(("dp", "row"), "col"), P("row", "col"), P(("dp", "row"), "col")),
        out_specs=(P(("dp", "row"), "col"), P(("dp", "row"), "col"), P(("row", "dp"), "col")),
        check_vma=False,
    )
```
